32 devices in a mesh: dp: 8 (over y, x, core), mp: 4 (over z).
Axes of the slice: x: 2, y: 2, z: 4, core: 2. Of those that a mesh axis runs over, the one named last changes fastest.
Arguments:
- token_ids: int32 [16, 16], replicated, may hold values from 0 to 64511
- prompt_lengths: int32 [16], replicated, may hold values from 128 to 6144, as said below
- cache_codes: bfloat16 [16, 6144, 2, 1024], P('dp', 'mp'), may hold values from -1 to 1
- cache_scales: bfloat16 [16, 48, 2, 1024], P('dp', 'mp'), may hold values from 0.03 to 400
- embedding: bfloat16 [64512, 8192], P('mp', 'dp'), may hold values from -12 to 12
- norm_gain: bfloat16 [8192], P('dp'), may hold values from 0.099609375 to 1.8984375
- query_weight: bfloat16 [8192, 8192], P('dp', 'mp'), may hold values from -0.0625 to 0.0625
- key_value_weight: bfloat16 [8192, 2, 1024], P('dp'), may hold values from -0.0625 to 0.0625
- output_weight: bfloat16 [8192, 8192], P('mp', 'dp'), may hold values from -0.0625 to 0.0625
Outputs:
- layer_out: bfloat16 [16, 16, 8192], P(None, None, 'dp')
The draws below stay inside these ranges and needn't reach their ends.
Inputs may be any that keep to these rules, and one draw needn't show every extreme that they name: `prompt_lengths`: each a multiple of 128; some row has exactly 6144 in every draw.
All inputs are finite; a program needn't handle non-finite values.
Results may differ from the reference program's by a relative error of at most 0.0065.
The reference program's roundings to bfloat16 on the way (of `scaled`, `cache`, `weights` and `mixed`) count: a program that leaves them out, or rounds other values in their place, can miss the bound.
Values may be sent and summed in bfloat16 or wider, within the bound.
No kernel may reach another device: no remote copies, remote signals or barrier semaphores. Data moves between devices by JAX's collectives and lax.ppermute only.
A program may use at most 192 MiB of HBM per device.

```python
import math
import jax
import jax.numpy as jnp
from jax import lax

D = 8192
QH = 64
KVH = 8
HEAD = 128
VOCAB = 64512
STORED_LENGTH = 6144
FACTOR_GROUP = 128
NEW = 16
QUESTION_COUNT = 16


def draw_prompt_lengths(key, part):
    first_key = jax.random.fold_in(key, 11)
    latter_entry_place = jax.random.fold_in(key, 12)
    blocks = jax.random.randint(first_key, (QUESTION_COUNT,), 1, STORED_LENGTH // FACTOR_GROUP + 1)
    longest = jax.random.randint(latter_entry_place, (), 0, QUESTION_COUNT)
    blocks = jnp.where(jnp.arange(QUESTION_COUNT) == longest, STORED_LENGTH // FACTOR_GROUP, blocks)
    return (blocks * FACTOR_GROUP).astype(jnp.int32)


def draw_cache_scales(key, part):
    first_key = jax.random.fold_in(key, 21)
    shape = (QUESTION_COUNT, STORED_LENGTH // FACTOR_GROUP, 2, KVH * HEAD)
    return jnp.exp(jax.random.uniform(first_key, shape, jnp.float32, math.log(0.03), math.log(3.0))).astype(jnp.bfloat16)


def draw_embedding(key, part):
    first_key = jax.random.fold_in(key, 31)
    latter_entry_place = jax.random.fold_in(key, 32)
    third_key = jax.random.fold_in(key, 33)
    beginning_shift = jnp.clip(jax.random.normal(first_key, (VOCAB, D), jnp.float32), -4.0, 4.0)
    row_scale = jnp.exp(jax.random.uniform(latter_entry_place, (VOCAB, 1), jnp.float32, math.log(0.1), 0.0))
    column_scale = jnp.exp(jax.random.uniform(third_key, (1, D), jnp.float32, math.log(0.3), math.log(3.0)))
    return (beginning_shift * row_scale * column_scale).astype(jnp.bfloat16)


def with_ends(drawn, key, least, largest):
    place = [jax.random.randint(jax.random.fold_in(key, axis), (), 0, length) for axis, length in enumerate(drawn.shape)]
    widest = drawn.shape.index(max(drawn.shape))
    next_to = place[:widest] + [(place[widest] + 1) % drawn.shape[widest]] + place[widest + 1:]
    return drawn.at[tuple(place)].set(least).at[tuple(next_to)].set(largest)


def block_scale(own_key, shape, pieces, low, high):
    def one(axis_at, shards_of):
        draws = jax.random.uniform(jax.random.fold_in(jax.random.fold_in(own_key, 6), axis_at), (shards_of,), jnp.float32, low / len(pieces), high / len(pieces))
        return jnp.repeat(jnp.exp(draws), shape[axis_at] // shards_of).reshape((-1,) + (1,) * (len(shape) - axis_at - 1))

    factor_of = one(*pieces[0])
    for cut in pieces[1:]:
        factor_of = factor_of * one(*cut)
    return factor_of


def centred(stream_key, extent, scale, limit, cuts=(), kind=jnp.bfloat16):
    entries = jax.random.normal(stream_key, extent, jnp.float32) * scale
    if len(cuts) > 0:
        entries = block_scale(stream_key, extent, cuts, -0.22, 0.18) * entries
    return jnp.clip(entries, min=-limit, max=limit).astype(kind)


def setup_inputs(seed: int = 0) -> dict:
    key_list = jax.random.split(jax.random.key(seed), 10)
    return {
        "token_ids": with_ends(jax.random.randint(key_list[0], (QUESTION_COUNT, NEW), 0, VOCAB), jax.random.fold_in(key_list[0], 1), 0, VOCAB - 1).astype(jnp.int32),
        "prompt_lengths": draw_prompt_lengths(jax.random.fold_in(key_list[9], 71), 0),
        "cache_codes": jnp.clip(jax.random.uniform(key_list[2], (QUESTION_COUNT, STORED_LENGTH, 2, KVH * HEAD), jnp.float32, -1.0, 1.0) * block_scale(key_list[2], (QUESTION_COUNT, STORED_LENGTH, 2, KVH * HEAD), ((0, 8), (1, 4)), -0.4, 0.0), -1.0, 1.0).astype(jnp.bfloat16),
        "cache_scales": draw_cache_scales(jax.random.fold_in(key_list[9], 71), 0),
        "embedding": draw_embedding(jax.random.fold_in(key_list[9], 71), 0),
        "norm_gain": jnp.clip(1.0 + 0.18 * jax.random.normal(key_list[5], (D,), jnp.float32), 0.099609375, 1.8984375).astype(jnp.bfloat16),
        "query_weight": centred(key_list[6], (D, QH * HEAD), D ** -0.5, 0.0625, ((0, 8), (1, 4))),
        "key_value_weight": centred(key_list[7], (D, 2, KVH * HEAD), D ** -0.5, 0.0625, ((0, 8),)),
        "output_weight": centred(key_list[8], (QH * HEAD, D), (QH * HEAD) ** -0.5, 0.0625, ((0, 4), (1, 8))),
    }


ROPE_BASE = 500000.0
EPSILON = 1e-05

def rotate(values, positions):
    width = values.shape[-1]
    half_width = width // 2
    exponent = jnp.arange(half_width, dtype=jnp.float32) * (2.0 / width)
    rates = jnp.exp(-jnp.log(ROPE_BASE) * exponent)
    angles = positions[..., None].astype(jnp.float32) * rates
    cosine = jnp.cos(angles)
    sinus_term = jnp.sin(angles)
    first = values[..., :half_width]
    second = values[..., half_width:]
    return jnp.concatenate([first * cosine - second * sinus_term, second * cosine + first * sinus_term], axis=-1)

def attend_row(queries, cache, new_keys, new_values, length):
    keys = jnp.concatenate([cache[:, 0], new_keys], axis=0).astype(jnp.float32)
    values = jnp.concatenate([cache[:, 1], new_values], axis=0).astype(jnp.float32)
    scores = jnp.einsum('tkgd,skd->kgts', queries.astype(jnp.float32), keys) * HEAD ** (-0.5)
    slots = jnp.arange(STORED_LENGTH + NEW, dtype=jnp.int32)
    steps = jnp.arange(NEW, dtype=jnp.int32)
    allowed = jnp.where(slots[None, :] < STORED_LENGTH, slots[None, :] < length, slots[None, :] - STORED_LENGTH <= steps[:, None])
    scores = jnp.where(allowed, scores, -jnp.inf)
    top = lax.optimization_barrier(jnp.max(scores, axis=-1, keepdims=True))
    lifted = jnp.exp(scores - top)
    weights = (lifted / lax.optimization_barrier(jnp.sum(lifted, axis=-1, keepdims=True))).astype(jnp.bfloat16)
    mixed = jnp.einsum('kgts,skd->tkgd', weights.astype(jnp.float32), values)
    return mixed.astype(jnp.bfloat16)

def reference(token_ids, prompt_lengths, cache_codes, cache_scales, embedding, norm_gain, query_weight, key_value_weight, output_weight):
    group = QH // KVH
    embedded = jnp.take(embedding, token_ids.reshape(-1), axis=0).astype(jnp.float32)
    scaled = (embedded * norm_gain.astype(jnp.float32)).astype(jnp.bfloat16)
    inverse = lax.rsqrt(lax.optimization_barrier(jnp.sum(embedded * embedded, axis=1)) / D + EPSILON)[:, None]
    queries = jnp.dot(scaled, query_weight, preferred_element_type=jnp.float32) * inverse
    fresh = jnp.dot(scaled, key_value_weight.reshape(D, 2 * KVH * HEAD), preferred_element_type=jnp.float32) * inverse
    positions = (prompt_lengths[:, None] + jnp.arange(NEW, dtype=jnp.int32)[None, :])[:, :, None]
    queries = rotate(queries.reshape(QUESTION_COUNT, NEW, QH, HEAD), positions).astype(jnp.bfloat16)
    queries = queries.reshape(QUESTION_COUNT, NEW, KVH, group, HEAD)
    fresh = fresh.reshape(QUESTION_COUNT, NEW, 2, KVH, HEAD)
    new_keys = rotate(fresh[:, :, 0], positions).astype(jnp.bfloat16)
    new_values = fresh[:, :, 1].astype(jnp.bfloat16)

    def one_row(items):
        codes, scales, query_row, key_row, value_row, length = items
        widened = codes.astype(jnp.float32).reshape(STORED_LENGTH // FACTOR_GROUP, FACTOR_GROUP, 2, KVH * HEAD)
        cache = (widened * scales.astype(jnp.float32)[:, None]).astype(jnp.bfloat16).reshape(STORED_LENGTH, 2, KVH, HEAD)
        return attend_row(query_row, cache, key_row, value_row, length)
    mixed = lax.map(one_row, (cache_codes, cache_scales, queries, new_keys, new_values, prompt_lengths))
    mixed = mixed.reshape(QUESTION_COUNT * NEW, QH * HEAD)
    result = jnp.dot(mixed, output_weight, preferred_element_type=jnp.float32)
    return result.astype(jnp.bfloat16).reshape(QUESTION_COUNT, NEW, D)
```

```python
import functools

import jax
import jax.numpy as jnp
from jax import lax
from jax.experimental import pallas as pl
from jax.experimental.pallas import tpu as pltpu
from jax.sharding import PartitionSpec as P

D = 8192
QH = 64
KVH = 8
HEAD = 128
FACTOR_GROUP = 128
NEW = 16

ROPE_BASE = 500000.0
EPSILON = 1e-05
LOWEST = -1e30
VMEM_LIMIT = 40 * 1024 * 1024

WIRE_PROJECTION = jnp.float32
WIRE_VALUES = jnp.float32
WIRE_OUTPUT = jnp.float32


def swap(value, axis, k):
    return lax.ppermute(value, axis, [(i, i ^ k) for i in range(lax.axis_size(axis))])


def call(kernel, **options):
    limit = options.pop("limit", VMEM_LIMIT)
    return pl.pallas_call(
        kernel, compiler_params=pltpu.CompilerParams(vmem_limit_bytes=limit), **options
    )


def widen_kernel(cache_ref, scale_ref, key_ref, value_ref, held, plain, sems):
    heads = pl.num_programs(1)
    step = pl.program_id(0) * heads + pl.program_id(1)
    last = pl.num_programs(0) * heads - 1
    slot = lax.rem(step, 2)
    span = held.shape[1]

    def fetch(n, into):
        lanes = pl.ds(pl.multiple_of(lax.rem(n, heads) * HEAD, HEAD), HEAD)
        return pltpu.make_async_copy(
            cache_ref.at[lax.div(n, heads), :, :, lanes], held.at[into], sems.at[into]
        )

    @pl.when(step == 0)
    def _():
        fetch(step, slot).start()

    @pl.when(step < last)
    def _():
        fetch(step + 1, 1 - slot).start()

    fetch(step, slot).wait()
    rows = held.at[slot].reshape(2 * span, HEAD)
    for group in range(span // FACTOR_GROUP):
        place = plain.at[group % 2]
        place[...] = rows[pl.ds(2 * group * FACTOR_GROUP, 2 * FACTOR_GROUP), :].astype(jnp.float32)
        for which, out_ref in ((0, key_ref), (1, value_ref)):
            entries = place[pl.ds(which, FACTOR_GROUP, stride=2), :]
            scales = scale_ref[0, 0, which, group : group + 1, :]
            out_ref[0, 0, pl.ds(group * FACTOR_GROUP, FACTOR_GROUP), :] = (
                entries * scales
            ).astype(jnp.bfloat16)


def widen(cache_codes, cache_scales):
    rows, span = cache_codes.shape[:2]
    groups = span // FACTOR_GROUP
    scales = cache_scales.astype(jnp.float32).reshape(rows, groups, 2, KVH, HEAD)
    scales = scales.transpose(0, 3, 2, 1, 4)
    block = pl.BlockSpec((1, 1, span, HEAD), lambda r, h: (r, h, 0, 0))
    shape = jax.ShapeDtypeStruct((rows, KVH, span, HEAD), jnp.bfloat16)
    return call(
        widen_kernel,
        grid=(rows, KVH),
        in_specs=[
            pl.BlockSpec(memory_space=pl.ANY),
            pl.BlockSpec((1, 1, 2, groups, HEAD), lambda r, h: (r, h, 0, 0, 0)),
        ],
        out_specs=[block, block],
        out_shape=[shape, shape],
        scratch_shapes=[
            pltpu.VMEM((2, span, 2, HEAD), jnp.bfloat16),
            pltpu.VMEM((2, 2 * FACTOR_GROUP, HEAD), jnp.float32),
            pltpu.SemaphoreType.DMA((2,)),
        ],
        name="widen",
    )(cache_codes, scales)


def project_kernel(parts, place_ref, *refs):
    pieces = refs[:parts]
    gain_ref, query_ref, fresh_ref, near_ref, far_ref, scaled, squares = refs[parts:]
    n = pl.program_id(0)
    piece = pieces[0].shape[0]
    half = near_ref.shape[0]
    tile = query_ref.shape[1]
    tiles = pl.num_programs(0) - 1

    @pl.when(n == 0)
    def _():
        for k, piece_ref in enumerate(pieces):
            rows = pl.ds(pl.multiple_of((place_ref[0] ^ k) * piece, piece), piece)
            values = piece_ref[...].astype(jnp.float32)
            scaled[rows, :] = (values * gain_ref[...]).astype(jnp.bfloat16)
            total = jnp.sum(values * values, axis=1, keepdims=True)
            squares[rows, :] = jnp.broadcast_to(total, (piece, HEAD))
        near_ref[:, (tiles + 1) * tile :] = squares[:half, :]
        far_ref[:, (tiles + 1) * tile :] = squares[half:, :]

    def multiply(weights, columns):
        product = jnp.dot(scaled[...], weights, preferred_element_type=jnp.float32)
        near_ref[:, columns] = product[:half]
        far_ref[:, columns] = product[half:]

    for t in range(tiles):

        @pl.when(n == t)
        def _(t=t):
            multiply(query_ref[...], pl.ds(t * tile, tile))

    @pl.when(n == tiles)
    def _():
        multiply(fresh_ref[...], pl.ds(tiles * tile, tile))


def project(place, pieces, gain, query_weight, fresh_weight):
    parts = len(pieces)
    piece, width = pieces[0].shape
    tokens = parts * piece
    tile = fresh_weight.shape[1]
    tiles = query_weight.shape[1] // tile
    columns = (tiles + 1) * tile + HEAD
    shape = jax.ShapeDtypeStruct((tokens // 2, columns), jnp.float32)
    whole = pl.BlockSpec((tokens // 2, columns), lambda n, p: (0, 0))
    return call(
        functools.partial(project_kernel, parts),
        grid_spec=pltpu.PrefetchScalarGridSpec(
            num_scalar_prefetch=1,
            grid=(tiles + 1,),
            in_specs=[pl.BlockSpec((piece, width), lambda n, p: (0, 0))] * parts
            + [
                pl.BlockSpec((1, width), lambda n, p: (0, 0)),
                pl.BlockSpec((width, tile), lambda n, p: (0, jnp.minimum(n, tiles - 1))),
                pl.BlockSpec((width, tile), lambda n, p: (0, 0)),
            ],
            out_specs=[whole, whole],
            scratch_shapes=[
                pltpu.VMEM((tokens, width), jnp.bfloat16),
                pltpu.VMEM((tokens, HEAD), jnp.float32),
            ],
        ),
        out_shape=[shape, shape],
        name="project",
    )(place, *pieces, gain, query_weight, fresh_weight)


def finish_kernel(heads, rotated, *refs):
    cosine_ref, sine_ref, *sums, out_ref = refs
    total = sums[0][...].astype(jnp.float32)
    for part in sums[1:]:
        total = total + part[...].astype(jnp.float32)
    square_sum = total[:, heads * HEAD : heads * HEAD + 1]
    inverse = lax.rsqrt(square_sum / D + EPSILON)
    for head in range(heads):
        values = total[:, head * HEAD : (head + 1) * HEAD] * inverse
        if head < rotated:
            values = values * cosine_ref[...] + pltpu.roll(values, HEAD // 2, 1) * sine_ref[...]
        out_ref[:, head * HEAD : (head + 1) * HEAD] = values.astype(jnp.bfloat16)


def finish(heads, rotated, cosine, sine, sums):
    return call(
        functools.partial(finish_kernel, heads, rotated),
        out_shape=jax.ShapeDtypeStruct((sums[0].shape[0], heads * HEAD), jnp.bfloat16),
        name="finish",
    )(cosine, sine, *sums)


def angle_tables(positions):
    half_width = HEAD // 2
    exponent = jnp.arange(half_width, dtype=jnp.float32) * (2.0 / HEAD)
    rates = jnp.exp(-jnp.log(ROPE_BASE) * exponent)
    angles = positions[:, None].astype(jnp.float32) * rates
    cosine = jnp.cos(angles)
    sine = jnp.sin(angles)
    return (
        jnp.concatenate([cosine, cosine], axis=-1),
        jnp.concatenate([-sine, sine], axis=-1),
    )


def attend_kernel(
    group, numbers_ref, query_ref, new_key_ref, new_value_ref, key_ref, value_ref, out_ref
):
    place = numbers_ref[0]
    length = numbers_ref[1 + pl.program_id(1)]
    span = key_ref.shape[2]
    rows = group * NEW
    factor = HEAD ** (-0.5)
    contract_last = (((1,), (1,)), ((), ()))
    queries = jnp.concatenate(
        [query_ref[:, g * HEAD : (g + 1) * HEAD] for g in range(group)], axis=0
    )
    older = (
        lax.dot_general(
            queries, key_ref[0, 0], contract_last, preferred_element_type=jnp.float32
        )
        * factor
    )
    fresh = (
        lax.dot_general(
            queries, new_key_ref[...], contract_last, preferred_element_type=jnp.float32
        )
        * factor
    )
    slots = place * span + lax.broadcasted_iota(jnp.int32, (1, span), 1)
    older = jnp.where(slots < length, older, -jnp.inf)
    steps = lax.rem(lax.broadcasted_iota(jnp.int32, (rows, NEW), 0), NEW)
    fresh_allowed = (lax.broadcasted_iota(jnp.int32, (rows, NEW), 1) <= steps) & (place == 0)
    fresh = jnp.where(fresh_allowed, fresh, -jnp.inf)
    top = jnp.maximum(
        jnp.maximum(
            jnp.max(older, axis=1, keepdims=True), jnp.max(fresh, axis=1, keepdims=True)
        ),
        LOWEST,
    )
    older = jnp.exp(older - top)
    fresh = jnp.exp(fresh - top)
    total = jnp.sum(older, axis=1, keepdims=True) + jnp.sum(fresh, axis=1, keepdims=True)

    def weighted(weights, values):
        rounded = weights.astype(jnp.bfloat16)
        rest = (weights - rounded.astype(jnp.float32)).astype(jnp.bfloat16)
        return jnp.dot(rounded, values, preferred_element_type=jnp.float32) + jnp.dot(
            rest, values, preferred_element_type=jnp.float32
        )

    sums = weighted(older, value_ref[0, 0]) + weighted(fresh, new_value_ref[...])
    out_ref[0, 0, :rows, :] = sums.astype(out_ref.dtype)
    lane = lax.broadcasted_iota(jnp.int32, (rows, HEAD), 1)
    table = jnp.zeros((rows, HEAD), jnp.float32)
    for first, number in ((0, top), (3, total)):
        for part in range(3):
            rounded = number.astype(jnp.bfloat16).astype(jnp.float32)
            table = jnp.where(lane == first + part, rounded, table)
            number = number - rounded
    turned = table.T[:NEW, :]
    out_ref[0, 0, rows:, :rows] = turned.astype(out_ref.dtype)


def attend(numbers, slot, pair, per_device, packed, keys, values, wire):
    rows_local, _, span, _ = keys.shape
    local_heads = packed.shape[1] // HEAD - 2 * per_device
    group = local_heads // per_device
    rows = group * NEW

    def head(b, numbers_ref):
        return (numbers_ref[0] ^ slot) // pair * per_device + b

    cache = pl.BlockSpec((1, 1, span, HEAD), lambda b, r, n: (r, head(b, n), 0, 0))
    return call(
        functools.partial(attend_kernel, group),
        grid_spec=pltpu.PrefetchScalarGridSpec(
            num_scalar_prefetch=1,
            grid=(per_device, rows_local),
            in_specs=[
                pl.BlockSpec((NEW, group * HEAD), lambda b, r, n: (r, b)),
                pl.BlockSpec((NEW, HEAD), lambda b, r, n: (r, local_heads + b)),
                pl.BlockSpec((NEW, HEAD), lambda b, r, n: (r, local_heads + per_device + b)),
                cache,
                cache,
            ],
            out_specs=pl.BlockSpec((1, 1, rows + NEW, HEAD), lambda b, r, n: (b, r, 0, 0)),
        ),
        out_shape=jax.ShapeDtypeStruct((per_device, rows_local, rows + NEW, HEAD), wire),
        name="attend",
    )(numbers, packed, packed, packed, keys, values)


def mix_kernel(group, *refs):
    *parts, out_ref = refs
    rows = group * NEW
    for b in range(parts[0].shape[0]):
        for r in range(parts[0].shape[1]):
            tops, totals = [], []
            for part in parts:
                tail = part[b, r, rows:, :rows].astype(jnp.float32)
                tops.append(tail[0:1] + tail[1:2] + tail[2:3])
                totals.append(tail[3:4] + tail[4:5] + tail[5:6])
            largest = functools.reduce(jnp.maximum, tops)
            shares = [jnp.exp(top - largest) for top in tops]
            whole = functools.reduce(jnp.add, [s * t for s, t in zip(shares, totals)])
            line = lax.broadcasted_iota(jnp.int32, (HEAD, rows), 0)
            table = jnp.zeros((HEAD, rows), jnp.float32)
            for n, share in enumerate(shares):
                table = jnp.where(line == n, share / whole, table)
            table = table.T
            total = jnp.zeros((rows, HEAD), jnp.float32)
            for n, part in enumerate(parts):
                total = total + part[b, r, :rows, :].astype(jnp.float32) * table[:, n : n + 1]
            total = total.astype(jnp.bfloat16)
            for g in range(group):
                lanes = pl.ds((b * group + g) * HEAD, HEAD)
                out_ref[pl.ds(r * NEW, NEW), lanes] = total[g * NEW : (g + 1) * NEW]


def mix(parts):
    per_device, rows_local, height, _ = parts[0].shape
    group = height // NEW - 1
    return call(
        functools.partial(mix_kernel, group),
        out_shape=jax.ShapeDtypeStruct(
            (rows_local * NEW, per_device * group * HEAD), jnp.bfloat16
        ),
        name="mix",
    )(*parts)


def deliver_kernel(blocks, parts, numbers_ref, *refs):
    mixed = refs[:blocks]
    weight_ref = refs[blocks]
    outs = refs[blocks + 1 : blocks + 1 + parts]
    gathered = refs[-1]
    piece = outs[0].shape[0]
    height = mixed[0].shape[0]
    step = min(height, piece)

    @pl.when(pl.program_id(0) == 0)
    def _():
        for s, block in enumerate(mixed):
            for part in range(height // step):
                token = (numbers_ref[1] ^ s) * height + part * step
                row = (lax.div(token, piece) ^ numbers_ref[0]) * piece + lax.rem(token, piece)
                gathered[pl.ds(pl.multiple_of(row, step), step), :] = block[
                    part * step : (part + 1) * step, :
                ]

    product = jnp.dot(gathered[...], weight_ref[...], preferred_element_type=jnp.float32)
    for k, out_ref in enumerate(outs):
        out_ref[...] = product[k * piece : (k + 1) * piece].astype(out_ref.dtype)


def deliver(numbers, mixed, weight, parts):
    blocks = len(mixed)
    height, depth = mixed[0].shape
    tokens = blocks * height
    piece = tokens // parts
    columns = weight.shape[1]
    tile = min(256, columns)
    return call(
        functools.partial(deliver_kernel, blocks, parts),
        grid_spec=pltpu.PrefetchScalarGridSpec(
            num_scalar_prefetch=1,
            grid=(columns // tile,),
            in_specs=[pl.BlockSpec((height, depth), lambda n, p: (0, 0))] * blocks
            + [pl.BlockSpec((depth, tile), lambda n, p: (0, n))],
            out_specs=[pl.BlockSpec((piece, tile), lambda n, p: (0, n))] * parts,
            scratch_shapes=[pltpu.VMEM((tokens, depth), jnp.bfloat16)],
        ),
        out_shape=[
            jax.ShapeDtypeStruct((piece, columns), WIRE_OUTPUT if k else jnp.float32)
            for k in range(parts)
        ],
        name="deliver",
    )(numbers, *mixed, weight)


def assemble_kernel(numbers_ref, *refs):
    *pieces, out_ref = refs
    height = pieces[0].shape[0]
    for k, piece in enumerate(pieces):
        row = pl.multiple_of((numbers_ref[0] ^ k) * height, height)
        out_ref[pl.ds(row, height), :] = piece[...]


def assemble(numbers, pieces):
    height, columns = pieces[0].shape
    return call(
        assemble_kernel,
        grid_spec=pltpu.PrefetchScalarGridSpec(
            num_scalar_prefetch=1,
            grid=(1,),
            in_specs=[pl.BlockSpec((height, columns), lambda n, p: (0, 0))] * len(pieces),
            out_specs=pl.BlockSpec((len(pieces) * height, columns), lambda n, p: (0, 0)),
        ),
        out_shape=jax.ShapeDtypeStruct((len(pieces) * height, columns), pieces[0].dtype),
        name="assemble",
    )(numbers, *pieces)


def on_device(
    token_ids,
    prompt_lengths,
    cache_codes,
    cache_scales,
    embedding,
    norm_gain,
    query_weight,
    key_value_weight,
    output_weight,
):
    parts = lax.axis_size("mp")
    groups = lax.axis_size("dp")
    place = lax.axis_index("mp")
    row_place = lax.axis_index("dp")
    pair = max(parts // KVH, 1)
    per_device = max(KVH // parts, 1)
    rows_local = cache_codes.shape[0]
    vocab_local = embedding.shape[0]
    local_heads = query_weight.shape[1] // HEAD
    tokens = token_ids.size
    block = rows_local * NEW
    piece = tokens // parts
    lengths = lax.dynamic_slice_in_dim(prompt_lengths, row_place * rows_local, rows_local)
    numbers = jnp.stack([place, row_place]).astype(jnp.int32)

    keys, values = widen(cache_codes, cache_scales)

    order = jnp.array([*range(0, groups, 2), *range(1, groups, 2)], jnp.int32)
    ids = token_ids.reshape(groups, block)[row_place ^ order].reshape(parts, piece)
    ids = ids[place ^ jnp.arange(parts, dtype=jnp.int32)].reshape(-1) - place * vocab_local
    inside = (ids >= 0) & (ids < vocab_local)
    picked = jnp.take(embedding, jnp.clip(ids, 0, vocab_local - 1), axis=0)
    picked = jnp.where(inside[:, None], picked, jnp.zeros((), picked.dtype))
    chunk = picked[:piece]
    for k in range(1, parts):
        chunk = chunk + swap(picked[k * piece : (k + 1) * piece], "mp", k)
    pieces = [chunk] + [swap(chunk, "mp", k) for k in range(1, parts)]

    first_head = place // pair * per_device
    fresh_weight = lax.dynamic_slice_in_dim(
        key_value_weight, first_head * HEAD, per_device * HEAD, axis=2
    ).reshape(key_value_weight.shape[0], 2 * per_device * HEAD)
    gain = norm_gain.astype(jnp.float32)[None, :]
    near, far = project(numbers, pieces, gain, query_weight, fresh_weight)
    near = near + swap(far, "dp", 1)
    sums = [near[:block]]
    for n in range(1, groups // 2):
        part = near[n * block : (n + 1) * block].astype(WIRE_PROJECTION)
        sums.append(swap(part, "dp", 2 * n))
    positions = (lengths[:, None] + jnp.arange(NEW, dtype=jnp.int32)[None, :]).reshape(-1)
    cosine, sine = angle_tables(positions)
    heads = local_heads + 2 * per_device
    packed = finish(heads, local_heads + per_device, cosine, sine, sums)

    slots = [packed] + [swap(packed, "mp", k) for k in range(1, parts)]
    attend_numbers = jnp.concatenate([numbers[:1], lengths])
    sums = []
    for k in range(parts):
        wire = WIRE_VALUES if k else jnp.float32
        part = attend(attend_numbers, k, pair, per_device, slots[k], keys, values, wire)
        sums.append(swap(part, "mp", k) if k else part)
    mixed = mix(sums)

    near_blocks = [mixed] + [swap(mixed, "dp", k) for k in range(2, groups, 2)]
    blocks = []
    for held in near_blocks:
        blocks += [held, swap(held, "dp", 1)]
    own, *others = deliver(numbers, blocks, output_weight, parts)
    for k, other in enumerate(others):
        own = own + swap(other, "mp", k + 1).astype(jnp.float32)
    own = own.astype(jnp.bfloat16)
    pieces = [own] + [swap(own, "mp", k) for k in range(1, parts)]
    result = assemble(numbers, pieces)
    return result.reshape(token_ids.shape[0], token_ids.shape[1], output_weight.shape[1])


def solution(mesh):
    return jax.shard_map(
        on_device,
        mesh=mesh,
        in_specs=(
            P(),
            P(),
            P("dp", "mp", None, None),
            P("dp", "mp", None, None),
            P("mp", "dp"),
            P("dp"),
            P("dp", "mp"),
            P("dp", None, None),
            P("mp", "dp"),
        ),
        out_specs=P(None, None, "dp"),
        check_vma=False,
    )
```
